512 devices in a mesh: section: 4 (over z_lo), dp: 16 (over z_hi, x, core), tensor: 8 (over y).
Axes of the slice: x: 4, y: 8, z: 8 (z_hi: 2, z_lo: 4; z = z_hi * 4 + z_lo), core: 2. Of those that a mesh axis runs over, the one named last changes fastest.
Arguments:
- inputs: bfloat16 [2048, 4096], P('dp'), may hold values from -5.625 to 5.625
- cotangent: bfloat16 [2048, 4096], P('dp'), may hold values from -5.625 to 5.625
- weights: bfloat16 [4, 4096, 4096], P('section', 'tensor', 'dp'), may hold values from -0.0625 to 0.5625
- gains: bfloat16 [4, 4096], P('section'), may hold values from 0.099609375 to 1.8984375
- stored: bfloat16 [3, 64, 64, 4096], P(None, 'dp', None, 'tensor'), may hold values from -5.625 to 5.625
- scale_exp: int32 [3, 64, 128], P(None, 'dp', 'tensor'), may hold values from -2 to 1
- example_ids: int32 [32], P('dp'), may hold values from 0 to 3
Outputs:
- section_outputs: bfloat16 [4, 2048, 4096], P('section', 'dp', 'tensor')
- input_grads: bfloat16 [4, 2048, 4096], P('section', 'dp', 'tensor')
- weight_grads: float32 [4, 4096, 4096], P('section', 'tensor', 'dp')
The draws below stay inside these ranges and needn't reach their ends.
Inputs may be any that keep to these rules, and one draw needn't show every extreme that they name: `example_ids`: ids index within their own data rank's 4 stored examples.
All inputs are finite; a program needn't handle non-finite values.
Results may differ from the reference program's by a relative error of at most 0.02.
Values may be sent and summed in bfloat16 or wider, within the bound.
No kernel may reach another device: no remote copies, remote signals or barrier semaphores. Data moves between devices by JAX's collectives and lax.ppermute only.
A program may use at most 64 MiB of HBM per device.

```python
import jax
import jax.numpy as jnp
from jax import lax

D = 4096
BLOCK = 32
WIN = 64
MICRO = 2
BUF = 4
BOUNDS = 3
TOKENS = 2048
EXAMPLES = 64
N_SECTION = 4
N_DP = 16
N_TENSOR = 8


def common_part(key):
    return jax.random.truncated_normal(key, -4.0, 4.0, (N_DP, 1, WIN, D), jnp.float32)


def draw_inputs(key, part):
    shared = common_part(key)
    key = jax.random.fold_in(key, 11)
    extent = (N_DP, MICRO, WIN, D)
    private = jax.random.truncated_normal(key, -4.0, 4.0, extent, jnp.float32)
    blended = 0.8 * shared + 0.6 * private
    return blended.reshape(N_DP * MICRO * WIN, D).astype(jnp.bfloat16)


def draw_cotangent(key, part):
    shared = common_part(key)
    key = jax.random.fold_in(key, 13)
    extent = (N_DP, MICRO, WIN, D)
    private = jax.random.truncated_normal(key, -4.0, 4.0, extent, jnp.float32)
    blended = 0.7 * shared + 0.7 * private
    return blended.reshape(N_DP * MICRO * WIN, D).astype(jnp.bfloat16)


def draw_stored(key, part):
    shared = common_part(key)
    key = jax.random.fold_in(key, 15)
    extent = (N_SECTION - 1, N_DP, BUF, WIN, D)
    private = jax.random.truncated_normal(key, -4.0, 4.0, extent, jnp.float32)
    blended = 0.7 * shared[None] + 0.7 * private
    return blended.reshape(N_SECTION - 1, N_DP * BUF, WIN, D).astype(jnp.bfloat16)


def draw_weights(key, part):
    key = jax.random.fold_in(key, 17)
    extent = (N_SECTION, D, D)
    private = jax.random.truncated_normal(key, -4.0, 4.0, extent, jnp.float32)
    diagonal_part = 0.5 * jnp.eye(D, dtype=jnp.float32)
    return (diagonal_part[None] + private * D ** (-0.5)).astype(jnp.bfloat16)


def plant(array, own_key, least, high):
    place = [jax.random.randint(jax.random.fold_in(own_key, axis), (), 0, length) for axis, length in enumerate(array.shape)]
    widest = array.shape.index(max(array.shape))
    next_to = place[:widest] + [(place[widest] + 1) % array.shape[widest]] + place[widest + 1:]
    return array.at[tuple(place)].set(least).at[tuple(next_to)].set(high)


def setup_inputs(seed: int = 0) -> dict:
    key_list = jax.random.split(jax.random.key(seed), 8)
    return {
        "inputs": draw_inputs(jax.random.fold_in(key_list[7], 71), 0),
        "cotangent": draw_cotangent(jax.random.fold_in(key_list[7], 71), 0),
        "weights": draw_weights(jax.random.fold_in(key_list[7], 71), 0),
        "gains": jnp.clip(1.0 + 0.18 * jax.random.normal(key_list[3], (N_SECTION, D), jnp.float32), 0.099609375, 1.8984375).astype(jnp.bfloat16),
        "stored": draw_stored(jax.random.fold_in(key_list[7], 71), 0),
        "scale_exp": plant(jax.random.randint(key_list[5], (BOUNDS, EXAMPLES, D // BLOCK), -2, 2), jax.random.fold_in(key_list[5], 1), -2, 1).astype(jnp.int32),
        "example_ids": plant(jax.random.randint(key_list[6], (N_DP * MICRO,), 0, BUF), jax.random.fold_in(key_list[6], 1), 0, BUF - 1).astype(jnp.int32),
    }


EPSILON = 1e-05

def settle(value):
    return lax.optimization_barrier(value.astype(jnp.bfloat16)).astype(jnp.float32)

def weight_sum(hidden, upstream):
    hidden_ranks = hidden.reshape(N_DP, MICRO * WIN, D)
    grad_ranks = upstream.reshape(N_DP, MICRO * WIN, D)

    def absorb(total, pair):
        product = jnp.dot(pair[0].T, pair[1], preferred_element_type=jnp.float32)
        return (total + settle(product), None)
    total, _ = lax.scan(absorb, jnp.zeros((D, D), jnp.float32), (hidden_ranks, grad_ranks))
    return total

def reference(inputs, cotangent, weights, gains, stored, scale_exp, example_ids):
    ranks = jnp.arange(N_DP * MICRO, dtype=jnp.int32) // MICRO
    chosen = (ranks * BUF + example_ids).astype(jnp.int32)
    group = D // N_TENSOR
    layer_in = inputs
    outputs = []
    saved = []
    for section_no in range(N_SECTION):
        values = layer_in.astype(jnp.float32)
        rstd = lax.rsqrt(lax.optimization_barrier(jnp.mean(values * values, axis=1, keepdims=True)) + EPSILON)
        normed = values * rstd
        hidden = (normed * gains[section_no].astype(jnp.float32)).astype(jnp.bfloat16)
        summed = jnp.zeros((TOKENS, D), jnp.float32)
        for group_no in range(N_TENSOR):
            lower = group_no * group
            product = jnp.dot(hidden[:, lower:lower + group], weights[section_no, lower:lower + group, :], preferred_element_type=jnp.float32)
            summed = summed + settle(product)
        result = values + summed
        outputs.append(result.astype(jnp.bfloat16))
        saved.append((hidden, normed, rstd))
        if section_no < N_SECTION - 1:
            previous = jnp.take(stored[section_no], chosen, axis=0).reshape(TOKENS, D).astype(jnp.float32)
            exponent = jnp.take(scale_exp[section_no], chosen, axis=0).astype(jnp.float32)
            limit = jnp.repeat(jnp.repeat(jnp.exp2(exponent), BLOCK, axis=1), WIN, axis=0)
            coded = jnp.clip(result - previous, -limit, limit)
            layer_in = (previous + settle(coded)).astype(jnp.bfloat16)
    grads = [None] * N_SECTION
    wgrads = [None] * N_SECTION
    upstream = cotangent
    for section_no in reversed(range(N_SECTION)):
        hidden, normed, rstd = saved[section_no]
        grad_hidden = jnp.dot(upstream, weights[section_no].T, preferred_element_type=jnp.float32)
        grad_normed = grad_hidden * gains[section_no].astype(jnp.float32)
        stat = lax.optimization_barrier(jnp.sum(grad_normed * normed, axis=1, keepdims=True)) / D
        grad_in = (upstream.astype(jnp.float32) + rstd * (grad_normed - normed * stat)).astype(jnp.bfloat16)
        grads[section_no] = grad_in
        wgrads[section_no] = weight_sum(hidden, upstream)
        upstream = grad_in
    return (jnp.stack(outputs), jnp.stack(grads), jnp.stack(wgrads))
```

```python
import jax
import jax.numpy as jnp
from jax import lax
from jax.experimental import pallas as pl
from jax.experimental.pallas import tpu as pltpu
from jax.sharding import PartitionSpec as P

BLOCK = 32
EPSILON = 1e-05
SIDE = 16
VMEM_LIMIT = 12 * 1024 * 1024
F32 = jnp.float32
BF16 = jnp.bfloat16


def split_row(row, width):
    tokens = row.shape[1]
    high = row.astype(BF16).astype(F32)
    parts = [high, row - high]
    if width > 2 * tokens:
        parts.append(jnp.zeros((1, width - 2 * tokens), F32))
    return jnp.concatenate(parts, axis=1)


def token_row(table):
    tokens, width = table.shape
    folded = table[:, :tokens]
    for start in range(tokens, width, tokens):
        folded = folded + table[:, start : start + tokens]
    return jnp.sum(folded.T, axis=0, keepdims=True)


def weight_specs(pieces):
    last = pieces[0].shape[0] - 1
    shape = (1, *pieces[0].shape[1:])
    here = pl.BlockSpec(shape, lambda i, flags: (jnp.where(flags[3] == 0, i, last - i), 0, 0, 0))
    there = pl.BlockSpec(shape, lambda i, flags: (jnp.where(flags[3] == 0, last - i, i), 0, 0, 0))
    return [here, there]


def project_kernel(flags, mine, theirs, first_mine, first_theirs, gain, *refs):
    here, there = refs[:2]
    cot = refs[2] if len(refs) == 7 else None
    out, raw, scaled, sums = refs[-4:]
    tokens, width = raw.shape
    local, piece = here.shape[-2:]
    first, core, flip = flags[0], flags[1], flags[2]

    @pl.when(pl.program_id(0) == 0)
    def _():
        for which, now, begin in ((core, mine, first_mine), (1 - core, theirs, first_theirs)):
            block = jnp.where(first == 1, begin[...], now[...])
            for half in range(2):
                start = pl.multiple_of(((half ^ flip) * 2 + which) * piece, piece)
                raw[:, pl.ds(start, piece)] = block[:, half * piece : (half + 1) * piece]
        values = raw[...].astype(F32)
        scaled[...] = (values * gain[...]).astype(BF16)
        upper = split_row(token_row(values * values), 2 * piece)
        lower = upper if cot is None else split_row(token_row(values * cot[...]), 2 * piece)
        index = lax.broadcasted_iota(jnp.int32, (SIDE, 2 * piece), 0)
        sums[...] = jnp.where(index < SIDE // 2, upper, lower).astype(BF16)

    def times(start, block):
        part = scaled[:, start : start + local]
        return jnp.dot(part, block, preferred_element_type=F32)

    out[0, :tokens, :piece] = (times(0, here[0, 0]) + times(local, here[0, 1])).astype(BF16)
    out[0, :tokens, piece:] = (times(0, there[0, 0]) + times(local, there[0, 1])).astype(BF16)
    out[0, tokens:, :] = sums[...]


def back_kernel(flags, chunk, here, there, *refs):
    total, sums = refs[-2:]
    rows = total.shape[0]
    local, piece = here.shape[-2:]
    core, flip = flags[1], flags[2]
    step = pl.program_id(0)

    @pl.when(step == 0)
    def _():
        total[...] = jnp.zeros_like(total)
        sums[...] = jnp.zeros_like(sums)

    def times(part, block):
        return lax.dot_general(part, block, (((1,), (1,)), ((), ())), preferred_element_type=F32)

    low, high = chunk[0, :rows, :piece], chunk[0, :rows, piece:]
    total[:, :local] += times(low, here[0, 0]) + times(high, there[0, 0])
    total[:, local:] += times(low, here[0, 1]) + times(high, there[0, 1])
    sums[...] += chunk[0, rows:, : 2 * rows].astype(F32)

    if len(refs) == 4:

        @pl.when(step == pl.num_programs(0) - 1)
        def _():
            mine, sent = refs[:2]
            for half in range(2):
                lanes = slice(half * piece, (half + 1) * piece)
                block = (half ^ flip) * 2
                start = pl.multiple_of((block + core) * piece, piece)
                mine[:, lanes] = total[:, pl.ds(start, piece)]
                start = pl.multiple_of((block + 1 - core) * piece, piece)
                sent[:rows, lanes] = total[:, pl.ds(start, piece)]
            both_parts = sums[:8, :rows] + sums[:8, rows:]
            sent[rows:, :rows] = both_parts
            if 2 * piece > rows:
                sent[rows:, rows:] = jnp.zeros((8, 2 * piece - rows), F32)


def whole_spec(value):
    return pl.BlockSpec(value.shape, lambda i, flags: (0,) * len(value.shape))


def project_call(flags, rows, gain, pieces, cot):
    tokens, own = rows[0].shape
    width = 2 * own
    ring, _, local, piece = pieces[0].shape
    operands = [*rows, gain, *pieces]
    specs = [whole_spec(value) for value in operands[:5]] + weight_specs(pieces)
    if cot is not None:
        operands.append(cot)
        specs.append(whole_spec(cot))
    return pl.pallas_call(
        project_kernel,
        grid_spec=pltpu.PrefetchScalarGridSpec(
            num_scalar_prefetch=1,
            grid=(ring,),
            in_specs=specs,
            out_specs=pl.BlockSpec((1, tokens + SIDE, 2 * piece), lambda i, flags: (i, 0, 0)),
            scratch_shapes=[
                pltpu.VMEM((tokens, width), BF16),
                pltpu.VMEM((tokens, width), BF16),
                pltpu.VMEM((SIDE, 2 * piece), BF16),
            ],
        ),
        out_shape=jax.ShapeDtypeStruct((ring, tokens + SIDE, 2 * piece), BF16),
        compiler_params=pltpu.CompilerParams(vmem_limit_bytes=VMEM_LIMIT),
        cost_estimate=pl.CostEstimate(
            flops=4 * tokens * width * piece * ring,
            bytes_accessed=2 * width * 2 * piece * ring,
            transcendentals=0,
        ),
    )(flags, *operands)


def back_call(flags, chunks, pieces, split):
    ring, _, local, piece = pieces[0].shape
    tokens = chunks.shape[1] - SIDE
    total = jax.ShapeDtypeStruct((tokens, 2 * local), F32)
    sums = jax.ShapeDtypeStruct((SIDE, 2 * tokens), F32)
    mine = jax.ShapeDtypeStruct((tokens, 2 * piece), F32)
    sent = jax.ShapeDtypeStruct((tokens + 8, 2 * piece), F32)
    outs = [mine, sent] if split else [total, sums]
    held = [total, sums] if split else []
    return pl.pallas_call(
        back_kernel,
        grid_spec=pltpu.PrefetchScalarGridSpec(
            num_scalar_prefetch=1,
            grid=(ring,),
            in_specs=[pl.BlockSpec((1, *chunks.shape[1:]), lambda i, flags: (i, 0, 0))]
            + weight_specs(pieces),
            out_specs=[whole_spec(value) for value in outs],
            scratch_shapes=[pltpu.VMEM(value.shape, F32) for value in held],
        ),
        out_shape=outs,
        compiler_params=pltpu.CompilerParams(vmem_limit_bytes=VMEM_LIMIT),
        cost_estimate=pl.CostEstimate(
            flops=8 * tokens * local * piece * ring,
            bytes_accessed=2 * local * 4 * piece * ring,
            transcendentals=0,
        ),
    )(flags, chunks, *pieces)


def side_rows(columns, width):
    rows = []
    for value in columns:
        high = lax.reduce_precision(value, 8, 7)
        pair = jnp.concatenate([high, value - high]).astype(BF16)
        rows.append(jnp.pad(pair, (0, width - pair.shape[0])))
    return jnp.pad(jnp.stack(rows), ((0, SIDE - len(rows)), (0, 0)))


def read_side(rows, tokens, row):
    pair = rows[:, row, : 2 * tokens].astype(F32)
    total = jnp.sum(pair, axis=0)
    return total[:tokens] + total[tokens:]


def ordered(flag, first, second, axis=0):
    return jnp.where(
        flag == 0, jnp.stack([first, second], axis), jnp.stack([second, first], axis)
    )


def body(inputs, cotangent, weights, gains, stored, scale_exp, example_ids):
    sections = lax.axis_size("section")
    ranks = lax.axis_size("dp")
    parts = lax.axis_size("tensor")
    section_pos = lax.axis_index("section")
    tensor_pos = lax.axis_index("tensor")
    dp_pos = lax.axis_index("dp")
    half = ranks // 2
    ring = half // 2
    quad = parts // 2
    z_half, x_pos, core = dp_pos // half, (dp_pos % half) // 2, dp_pos % 2
    y_half = tensor_pos // quad
    y_pos = jnp.where(y_half == 0, tensor_pos, parts - 1 - tensor_pos)
    flip = z_half ^ y_half
    tokens, width = inputs.shape
    local = weights.shape[1]
    piece = weights.shape[2]
    micro = example_ids.shape[0]
    window = tokens // micro
    bounds = stored.shape[0]
    is_first = section_pos == 0
    is_last = section_pos == sections - 1

    def rank_of(z, x, c):
        return z * half + x * 2 + c

    def row_of(h, q):
        return parts - 1 - q if h else q

    def quad_of(y):
        return (1, parts - 1 - y) if y >= quad else (0, y)

    def move(block, target):
        route = []
        for d in range(ranks):
            for y in range(parts):
                z, x, c, h, q = target(d // half, (d % half) // 2, d % 2, *quad_of(y))
                route.append((d * parts + y, rank_of(z, x, c) * parts + row_of(h, q)))
        return lax.ppermute(block, ("dp", "tensor"), route)

    def back_and_move(block, target):
        route = []
        for s in range(sections):
            for d in range(ranks):
                for y in range(parts):
                    z, x, c, h, q = target(d // half, (d % half) // 2, d % 2, *quad_of(y))
                    there = rank_of(z, x, c) * parts + row_of(h, q)
                    before = (s - 1) % sections
                    route.append(((s * ranks + d) * parts + y, before * ranks * parts + there))
        return lax.ppermute(block, ("section", "dp", "tensor"), route)

    def swap_z(block):
        return lax.ppermute(block, "dp", [(i, (i + half) % ranks) for i in range(ranks)])

    def swap_y(block):
        return lax.ppermute(block, "tensor", [(i, parts - 1 - i) for i in range(parts)])

    def swap_core(block):
        return lax.ppermute(block, "dp", [(i, i ^ 1) for i in range(ranks)])

    def turn(block):
        return move(block, lambda z, x, c, h, q: (z, x, h, c, q))

    def shift_x(block, step):
        route = [
            (rank_of(z, x, c), rank_of(z, (x + step) % ring, c))
            for z in range(2)
            for x in range(ring)
            for c in range(2)
        ]
        return lax.ppermute(block, "dp", route)

    def hop(block, step):
        devices = range(sections)
        return lax.ppermute(
            block, "section", [(i, i + step) for i in devices if i + step in devices]
        )

    def pass_on(z, to_z, x, c, h, q):
        to_x = ring - 1 - q if to_z else q
        return to_z, to_x, c, h, (to_x - x) % ring

    quads = [[row_of(h, i) for i in range(quad)] for h in range(2)]
    rings = [[rank_of(z, x, c) for x in range(ring)] for z in range(2) for c in range(2)]

    def exchange_quad(chunks):
        return lax.all_to_all(chunks, "tensor", 0, 0, axis_index_groups=quads)

    with jax.named_scope("weight_gather"):

        def gather_x(block):
            copies = jnp.broadcast_to(block[None], (ring, *block.shape))
            return lax.all_to_all(copies, "dp", 0, 0, axis_index_groups=rings)

        own_block = weights[0]
        by_y = swap_y(own_block)
        by_z = swap_z(own_block)
        by_both = swap_y(by_z)
        here = gather_x(jnp.stack([own_block, by_y]))
        by_both, here = lax.optimization_barrier((by_both, here))
    flags = jnp.stack([is_first.astype(jnp.int32), core, flip, z_half]).astype(jnp.int32)

    with jax.named_scope("layout"):
        native = core == y_half

        def blocks_of(rows):
            first = lax.dynamic_slice_in_dim(rows, tensor_pos * local, local, 1)
            second = lax.dynamic_slice_in_dim(rows, (parts - 1 - tensor_pos) * local, local, 1)
            return jnp.concatenate([first, second], axis=1)

        def columns_of(rows, which):
            table = rows.reshape(tokens, 2, ring, 2, piece)
            table = lax.dynamic_index_in_dim(table, which, 3, keepdims=False)
            low = jnp.stack([table[:, 0, i] for i in range(ring)])
            high = jnp.stack([table[:, 1, ring - 1 - i] for i in range(ring)])
            return ordered(z_half, low, high, axis=2).reshape(ring, tokens, 2 * piece)

        handed = (blocks_of(inputs), columns_of(cotangent, 1 - core))
        route = [
            (rank_of(z, x, h) * parts + row_of(h, q), rank_of(z, x, 1 - h) * parts + row_of(h, q))
            for z in range(2)
            for x in range(ring)
            for h in range(2)
            for q in range(quad)
        ]
        handed = [lax.ppermute(value, ("dp", "tensor"), route) for value in handed]
        first_rows = jnp.where(native, blocks_of(inputs), handed[0])
        cot_chunks = jnp.where(native, columns_of(cotangent, core), handed[1])
        own_cotangent = lax.dynamic_index_in_dim(cot_chunks, y_pos, 0, keepdims=False)

        def turned(table):
            return jnp.where(flip == 0, table, jnp.concatenate([table[:, 1:], table[:, :1]], axis=1))

        def own_of(rows, which):
            table = rows.reshape(rows.shape[0], 2, 2, piece)
            table = lax.dynamic_index_in_dim(table, which, 2, keepdims=False)
            return turned(table).reshape(rows.shape[0], 2 * piece)

        def rows_of(mine, other):
            table = ordered(
                core, mine.reshape(tokens, 2, piece), other.reshape(tokens, 2, piece), axis=2
            )
            return turned(table).reshape(tokens, 2 * local)

        gain_rows = blocks_of(gains).astype(F32)
        gain_own = own_of(gain_rows, core)

        bound = jnp.clip(section_pos, 0, bounds - 1)

        def chosen(table):
            return jnp.take(
                lax.dynamic_index_in_dim(table, bound, 0, keepdims=False), example_ids, axis=0
            )

        kept = chosen(stored).reshape(tokens, local)
        limit = jnp.repeat(jnp.exp2(chosen(scale_exp).astype(F32)), BLOCK, axis=1).astype(BF16)
        kept = jnp.concatenate([kept, jnp.pad(limit, ((0, SIDE - micro), (0, 0)))], axis=0)
        here, kept = lax.optimization_barrier((here, kept))
        kept = turn(kept).reshape(tokens + SIDE, 2, piece)
        mine = lax.dynamic_index_in_dim(kept, core, 1, keepdims=False)
        theirs = swap_core(lax.dynamic_index_in_dim(kept, 1 - core, 1, keepdims=False))
        kept = ordered(core ^ z_half, mine, theirs, axis=1).reshape(tokens + SIDE, 2 * piece)
        previous = kept[:tokens].astype(F32)
        limit = jnp.repeat(kept[tokens : tokens + micro].astype(F32), window, axis=0)
        there = gather_x(jnp.stack([by_z, by_both]))
        there, previous, limit = lax.optimization_barrier((there, previous, limit))
        pieces = (here, there)

    first_own, first_other = own_of(first_rows, core), own_of(first_rows, 1 - core)

    def place(owns):
        table = jnp.stack(owns).reshape(len(owns), tokens, 2, piece)
        side = core ^ z_half
        mine = lax.dynamic_index_in_dim(table, side, 2, keepdims=False)
        theirs = swap_core(lax.dynamic_index_in_dim(table, 1 - side, 2, keepdims=False))
        return turn(ordered(core, mine, theirs, axis=2).reshape(len(owns), tokens, local))

    cot_chunks = jnp.pad(cot_chunks, ((0, 0), (0, SIDE), (0, 0)))
    cot_part, _ = back_call(flags, cot_chunks, pieces, False)
    cot_normed = gain_rows * (cot_part + swap_core(cot_part))

    own, following, other = first_own, first_own, first_other

    def norm_of(total):
        return lax.rsqrt(total / width + EPSILON)[:, None]

    for tick_no in range(sections):
        finished = tick_no == sections - 1
        rows = (following, other, first_own, first_other)
        outgoing = project_call(flags, rows, gain_rows, pieces, cot_normed if finished else None)
        received = exchange_quad(outgoing)
        rstd = norm_of(read_side(received[:, tokens:], tokens, 0))
        change = rstd * jnp.sum(received[:, :tokens].astype(F32), axis=0)
        result = own.astype(F32) + change
        if not finished:
            coded = jnp.clip(result - previous, -limit, limit).astype(BF16)
            following = hop((previous + coded.astype(F32)).astype(BF16), 1)
            own = jnp.where(is_first, first_own, following)
            other = swap_core(following)
        if tick_no == 1:
            other, cot_normed = lax.optimization_barrier((other, cot_normed))
    section_output = result.astype(BF16)

    stat = read_side(received[:, tokens:], tokens, SIDE // 2)[:, None] * rstd / width
    normed = own.astype(F32) * rstd
    last_grad = own_cotangent.astype(F32) + rstd * (own_of(cot_normed, core) - normed * stat)
    last_grad = last_grad.astype(BF16)

    last_rows = jnp.where(is_first, first_rows, rows_of(following, other)).astype(F32)
    hidden = (last_rows * rstd * gain_rows).astype(BF16)
    hidden = lax.dynamic_slice_in_dim(hidden, core * (tokens // 2), tokens // 2, 0)
    hidden_near, hidden_far = hidden[:, :local], swap_y(hidden[:, local:])

    grad_in = last_grad
    for tick_no in range(1, sections):
        moved = hop(grad_in, -1)
        if tick_no == 1:
            moved, hidden_far = lax.optimization_barrier((moved, hidden_far))
            hidden = ordered(y_half, hidden_near, hidden_far)
        upstream = jnp.where(is_last, own_cotangent, moved)
        if tick_no == sections - 1:
            sent = jnp.where(is_first, own_cotangent, grad_in).reshape(tokens, 2, piece)
            same = back_and_move(sent[:, 0], lambda z, x, c, h, q: pass_on(z, z, x, c, h, q))
            cross = back_and_move(sent[:, 1], lambda z, x, c, h, q: pass_on(z, 1 - z, x, c, h, q))
            columns = ordered(z_half, same, cross)
        values = upstream.astype(F32)
        side = side_rows([jnp.sum(values * change, axis=1)], 2 * piece)
        payload = jnp.concatenate([upstream, side], axis=0)
        gathered = exchange_quad(jnp.broadcast_to(payload[None], (quad, *payload.shape)))
        if tick_no == 1:
            gathered, hidden_far = lax.optimization_barrier((gathered, swap_z(hidden)))
            hidden = ordered(z_half, hidden, hidden_far)
        elif tick_no == 2:
            found = [hidden] + [shift_x(hidden, step) for step in range(1, ring)]
            gathered, found = lax.optimization_barrier((gathered, found))
            hidden = jnp.stack(found)
        elif tick_no == 3:
            gathered, hidden_far = lax.optimization_barrier((gathered, swap_core(hidden)))
            hidden = ordered(core, hidden, hidden_far, axis=3)
            order = [hidden[i, :, 0] for i in range(ring)]
            order += [hidden[ring - 1 - i, :, 1] for i in range(ring)]
            hidden = jnp.stack(order).reshape(ranks * tokens, local)
        part_mine, sent = back_call(flags, gathered, pieces, True)
        sum_mine = sent[tokens, :tokens]
        taken = swap_core(sent)
        stat = (sum_mine + taken[tokens, :tokens])[:, None] / width
        grad_normed = gain_own * (part_mine + taken[:tokens])
        grad_in = values + rstd * (grad_normed - normed * stat)
        grad_in = jnp.where(is_last, last_grad, grad_in.astype(BF16))
    placed = place([section_output, grad_in])

    with jax.named_scope("weight_grad"):
        columns = lax.all_to_all(
            jnp.broadcast_to(columns[None], (parts, *columns.shape)), "tensor", 0, 0
        ).reshape(ranks * tokens, piece)
        weight_grad = lax.dot_general(
            hidden, columns, (((0,), (0,)), ((), ())), preferred_element_type=F32
        )
    return placed[:1], placed[1:], weight_grad[None]


def solution(mesh):
    return jax.shard_map(
        body,
        mesh=mesh,
        in_specs=(
            P("dp", None),
            P("dp", None),
            P("section", "tensor", "dp"),
            P("section", None),
            P(None, "dp", None, "tensor"),
            P(None, "dp", "tensor"),
            P("dp"),
        ),
        out_specs=(
            P("section", "dp", "tensor"),
            P("section", "dp", "tensor"),
            P("section", "tensor", "dp"),
        ),
        check_vma=False,
    )
```

```python
import jax
import jax.numpy as jnp
from jax import lax
from jax.experimental import pallas as pl
from jax.experimental.pallas import tpu as pltpu
from jax.sharding import PartitionSpec as P

BLOCK = 32
EPSILON = 1e-05
SIDE = 16
VMEM_LIMIT = 12 * 1024 * 1024
F32 = jnp.float32
BF16 = jnp.bfloat16


def split_row(row, width):
    tokens = row.shape[1]
    high = row.astype(BF16).astype(F32)
    parts = [high, row - high]
    if width > 2 * tokens:
        parts.append(jnp.zeros((1, width - 2 * tokens), F32))
    return jnp.concatenate(parts, axis=1)


def token_row(table):
    tokens, width = table.shape
    folded = table[:, :tokens]
    for start in range(tokens, width, tokens):
        folded = folded + table[:, start : start + tokens]
    return jnp.sum(folded.T, axis=0, keepdims=True)


def weight_specs(pieces):
    last = pieces[0].shape[0] - 1
    block = pieces[0].shape[1:]
    here = pl.BlockSpec((1, *block), lambda i, flags: (jnp.where(flags[3] == 0, i, last - i), 0, 0))
    there = pl.BlockSpec(
        (1, 2, *block), lambda i, flags: (jnp.where(flags[3] == 0, last - i, i), 0, 0, 0)
    )
    return [here, here, there]


def project_kernel(flags, mine, theirs, first_mine, first_theirs, gain, *refs):
    near, side, there = refs[:3]
    cot = refs[3] if len(refs) == 8 else None
    out, raw, scaled, sums = refs[-4:]
    tokens, width = raw.shape
    local, piece = near.shape[-2:]
    first, core, flip = flags[0], flags[1], flags[2]

    @pl.when(pl.program_id(0) == 0)
    def _():
        for which, now, begin in ((core, mine, first_mine), (1 - core, theirs, first_theirs)):
            block = jnp.where(first == 1, begin[...], now[...])
            for half in range(2):
                start = pl.multiple_of(((half ^ flip) * 2 + which) * piece, piece)
                raw[:, pl.ds(start, piece)] = block[:, half * piece : (half + 1) * piece]
        values = raw[...].astype(F32)
        scaled[...] = (values * gain[...]).astype(BF16)
        upper = split_row(token_row(values * values), 2 * piece)
        lower = upper if cot is None else split_row(token_row(values * cot[...]), 2 * piece)
        index = lax.broadcasted_iota(jnp.int32, (SIDE, 2 * piece), 0)
        sums[...] = jnp.where(index < SIDE // 2, upper, lower).astype(BF16)

    def times(start, block):
        part = scaled[:, start : start + local]
        return jnp.dot(part, block, preferred_element_type=F32)

    out[0, :tokens, :piece] = (times(0, near[0]) + times(local, side[0])).astype(BF16)
    out[0, :tokens, piece:] = (times(0, there[0, 0]) + times(local, there[0, 1])).astype(BF16)
    out[0, tokens:, :] = sums[...]


def back_kernel(flags, chunk, near, side, there, *refs):
    total, sums = refs[-2:]
    rows = total.shape[0]
    local, piece = near.shape[-2:]
    core, flip = flags[1], flags[2]
    step = pl.program_id(0)

    @pl.when(step == 0)
    def _():
        total[...] = jnp.zeros_like(total)
        sums[...] = jnp.zeros_like(sums)

    def times(part, block):
        return lax.dot_general(part, block, (((1,), (1,)), ((), ())), preferred_element_type=F32)

    low, high = chunk[0, :rows, :piece], chunk[0, :rows, piece:]
    total[:, :local] += times(low, near[0]) + times(high, there[0, 0])
    total[:, local:] += times(low, side[0]) + times(high, there[0, 1])
    sums[...] += chunk[0, rows:, : 2 * rows].astype(F32)

    if len(refs) == 4:

        @pl.when(step == pl.num_programs(0) - 1)
        def _():
            mine, sent = refs[:2]
            for half in range(2):
                lanes = slice(half * piece, (half + 1) * piece)
                block = (half ^ flip) * 2
                start = pl.multiple_of((block + core) * piece, piece)
                mine[:, lanes] = total[:, pl.ds(start, piece)]
                start = pl.multiple_of((block + 1 - core) * piece, piece)
                sent[:rows, lanes] = total[:, pl.ds(start, piece)]
            both_parts = sums[:8, :rows] + sums[:8, rows:]
            sent[rows:, :rows] = both_parts
            if 2 * piece > rows:
                sent[rows:, rows:] = jnp.zeros((8, 2 * piece - rows), F32)


def whole_spec(value):
    return pl.BlockSpec(value.shape, lambda i, flags: (0,) * len(value.shape))


def project_call(flags, rows, gain, pieces, cot):
    tokens, own = rows[0].shape
    width = 2 * own
    ring, local, piece = pieces[0].shape
    operands = [*rows, gain, *pieces]
    specs = [whole_spec(value) for value in operands[:5]] + weight_specs(pieces)
    if cot is not None:
        operands.append(cot)
        specs.append(whole_spec(cot))
    return pl.pallas_call(
        project_kernel,
        grid_spec=pltpu.PrefetchScalarGridSpec(
            num_scalar_prefetch=1,
            grid=(ring,),
            in_specs=specs,
            out_specs=pl.BlockSpec((1, tokens + SIDE, 2 * piece), lambda i, flags: (i, 0, 0)),
            scratch_shapes=[
                pltpu.VMEM((tokens, width), BF16),
                pltpu.VMEM((tokens, width), BF16),
                pltpu.VMEM((SIDE, 2 * piece), BF16),
            ],
        ),
        out_shape=jax.ShapeDtypeStruct((ring, tokens + SIDE, 2 * piece), BF16),
        compiler_params=pltpu.CompilerParams(vmem_limit_bytes=VMEM_LIMIT),
        cost_estimate=pl.CostEstimate(
            flops=4 * tokens * width * piece * ring,
            bytes_accessed=2 * width * 2 * piece * ring,
            transcendentals=0,
        ),
    )(flags, *operands)


def back_call(flags, chunks, pieces, split):
    ring, local, piece = pieces[0].shape
    tokens = chunks.shape[1] - SIDE
    total = jax.ShapeDtypeStruct((tokens, 2 * local), F32)
    sums = jax.ShapeDtypeStruct((SIDE, 2 * tokens), F32)
    mine = jax.ShapeDtypeStruct((tokens, 2 * piece), F32)
    sent = jax.ShapeDtypeStruct((tokens + 8, 2 * piece), F32)
    outs = [mine, sent] if split else [total, sums]
    held = [total, sums] if split else []
    return pl.pallas_call(
        back_kernel,
        grid_spec=pltpu.PrefetchScalarGridSpec(
            num_scalar_prefetch=1,
            grid=(ring,),
            in_specs=[pl.BlockSpec((1, *chunks.shape[1:]), lambda i, flags: (i, 0, 0))]
            + weight_specs(pieces),
            out_specs=[whole_spec(value) for value in outs],
            scratch_shapes=[pltpu.VMEM(value.shape, F32) for value in held],
        ),
        out_shape=outs,
        compiler_params=pltpu.CompilerParams(vmem_limit_bytes=VMEM_LIMIT),
        cost_estimate=pl.CostEstimate(
            flops=8 * tokens * local * piece * ring,
            bytes_accessed=2 * local * 4 * piece * ring,
            transcendentals=0,
        ),
    )(flags, chunks, *pieces)


def side_rows(columns, width):
    rows = []
    for value in columns:
        high = lax.reduce_precision(value, 8, 7)
        pair = jnp.concatenate([high, value - high]).astype(BF16)
        rows.append(jnp.pad(pair, (0, width - pair.shape[0])))
    return jnp.pad(jnp.stack(rows), ((0, SIDE - len(rows)), (0, 0)))


def read_side(rows, tokens, row):
    pair = rows[:, row, : 2 * tokens].astype(F32)
    total = jnp.sum(pair, axis=0)
    return total[:tokens] + total[tokens:]


def ordered(flag, first, second, axis=0):
    return jnp.where(
        flag == 0, jnp.stack([first, second], axis), jnp.stack([second, first], axis)
    )


def body(inputs, cotangent, weights, gains, stored, scale_exp, example_ids):
    sections = lax.axis_size("section")
    ranks = lax.axis_size("dp")
    parts = lax.axis_size("tensor")
    section_pos = lax.axis_index("section")
    tensor_pos = lax.axis_index("tensor")
    dp_pos = lax.axis_index("dp")
    half = ranks // 2
    ring = half // 2
    quad = parts // 2
    z_half, x_pos, core = dp_pos // half, (dp_pos % half) // 2, dp_pos % 2
    y_half = tensor_pos // quad
    y_pos = jnp.where(y_half == 0, tensor_pos, parts - 1 - tensor_pos)
    flip = z_half ^ y_half
    tokens, width = inputs.shape
    local = weights.shape[1]
    piece = weights.shape[2]
    micro = example_ids.shape[0]
    window = tokens // micro
    bounds = stored.shape[0]
    is_first = section_pos == 0
    is_last = section_pos == sections - 1

    def rank_of(z, x, c):
        return z * half + x * 2 + c

    def row_of(h, q):
        return parts - 1 - q if h else q

    def quad_of(y):
        return (1, parts - 1 - y) if y >= quad else (0, y)

    def move(block, target):
        route = []
        for d in range(ranks):
            for y in range(parts):
                z, x, c, h, q = target(d // half, (d % half) // 2, d % 2, *quad_of(y))
                route.append((d * parts + y, rank_of(z, x, c) * parts + row_of(h, q)))
        return lax.ppermute(block, ("dp", "tensor"), route)

    def back_and_move(block, target):
        route = []
        for s in range(sections):
            for d in range(ranks):
                for y in range(parts):
                    z, x, c, h, q = target(d // half, (d % half) // 2, d % 2, *quad_of(y))
                    there = rank_of(z, x, c) * parts + row_of(h, q)
                    before = (s - 1) % sections
                    route.append(((s * ranks + d) * parts + y, before * ranks * parts + there))
        return lax.ppermute(block, ("section", "dp", "tensor"), route)

    def swap_z(block):
        return lax.ppermute(block, "dp", [(i, (i + half) % ranks) for i in range(ranks)])

    def swap_y(block):
        return lax.ppermute(block, "tensor", [(i, parts - 1 - i) for i in range(parts)])

    def swap_core(block):
        return lax.ppermute(block, "dp", [(i, i ^ 1) for i in range(ranks)])

    def turn(block):
        return move(block, lambda z, x, c, h, q: (z, x, h, c, q))

    def shift_x(block, step):
        route = [
            (rank_of(z, x, c), rank_of(z, (x + step) % ring, c))
            for z in range(2)
            for x in range(ring)
            for c in range(2)
        ]
        return lax.ppermute(block, "dp", route)

    def hop(block, step):
        devices = range(sections)
        return lax.ppermute(
            block, "section", [(i, i + step) for i in devices if i + step in devices]
        )

    def pass_on(z, to_z, x, c, h, q):
        to_x = ring - 1 - q if to_z else q
        return to_z, to_x, c, h, (to_x - x) % ring

    quads = [[row_of(h, i) for i in range(quad)] for h in range(2)]
    rings = [[rank_of(z, x, c) for x in range(ring)] for z in range(2) for c in range(2)]

    def exchange_quad(chunks):
        return lax.all_to_all(chunks, "tensor", 0, 0, axis_index_groups=quads)

    with jax.named_scope("weight_gather"):

        def gather_x(block):
            copies = jnp.broadcast_to(block[None], (ring, *block.shape))
            return lax.all_to_all(copies, "dp", 0, 0, axis_index_groups=rings)

        own_block = weights[0]
        by_y = swap_y(own_block)
        by_z = swap_z(own_block)
        near = gather_x(own_block)
        by_y, near = lax.optimization_barrier((by_y, near))
        by_both = swap_y(by_z)
        side = gather_x(by_y)
        by_z, by_both, side = lax.optimization_barrier((by_z, by_both, side))
    flags = jnp.stack([is_first.astype(jnp.int32), core, flip, z_half]).astype(jnp.int32)

    with jax.named_scope("layout"):
        native = core == y_half

        def blocks_of(rows):
            first = lax.dynamic_slice_in_dim(rows, tensor_pos * local, local, 1)
            second = lax.dynamic_slice_in_dim(rows, (parts - 1 - tensor_pos) * local, local, 1)
            return jnp.concatenate([first, second], axis=1)

        def columns_of(rows, which):
            table = rows.reshape(tokens, 2, ring, 2, piece)
            table = lax.dynamic_index_in_dim(table, which, 3, keepdims=False)
            low = jnp.stack([table[:, 0, i] for i in range(ring)])
            high = jnp.stack([table[:, 1, ring - 1 - i] for i in range(ring)])
            return ordered(z_half, low, high, axis=2).reshape(ring, tokens, 2 * piece)

        handed = (blocks_of(inputs), columns_of(cotangent, 1 - core))
        route = [
            (rank_of(z, x, h) * parts + row_of(h, q), rank_of(z, x, 1 - h) * parts + row_of(h, q))
            for z in range(2)
            for x in range(ring)
            for h in range(2)
            for q in range(quad)
        ]
        handed = [lax.ppermute(value, ("dp", "tensor"), route) for value in handed]
        first_rows = jnp.where(native, blocks_of(inputs), handed[0])
        cot_chunks = jnp.where(native, columns_of(cotangent, core), handed[1])
        own_cotangent = lax.dynamic_index_in_dim(cot_chunks, y_pos, 0, keepdims=False)

        def turned(table):
            return jnp.where(flip == 0, table, jnp.concatenate([table[:, 1:], table[:, :1]], axis=1))

        def own_of(rows, which):
            table = rows.reshape(rows.shape[0], 2, 2, piece)
            table = lax.dynamic_index_in_dim(table, which, 2, keepdims=False)
            return turned(table).reshape(rows.shape[0], 2 * piece)

        def rows_of(mine, other):
            table = ordered(
                core, mine.reshape(tokens, 2, piece), other.reshape(tokens, 2, piece), axis=2
            )
            return turned(table).reshape(tokens, 2 * local)

        gain_rows = blocks_of(gains).astype(F32)
        gain_own = own_of(gain_rows, core)

        bound = jnp.clip(section_pos, 0, bounds - 1)

        def chosen(table):
            return jnp.take(
                lax.dynamic_index_in_dim(table, bound, 0, keepdims=False), example_ids, axis=0
            )

        kept = chosen(stored).reshape(tokens, local)
        limit = jnp.repeat(jnp.exp2(chosen(scale_exp).astype(F32)), BLOCK, axis=1).astype(BF16)
        kept = jnp.concatenate([kept, jnp.pad(limit, ((0, SIDE - micro), (0, 0)))], axis=0)
        side, kept = lax.optimization_barrier((side, kept))
        kept = turn(kept).reshape(tokens + SIDE, 2, piece)
        mine = lax.dynamic_index_in_dim(kept, core, 1, keepdims=False)
        theirs = swap_core(lax.dynamic_index_in_dim(kept, 1 - core, 1, keepdims=False))
        kept = ordered(core ^ z_half, mine, theirs, axis=1).reshape(tokens + SIDE, 2 * piece)
        previous = kept[:tokens].astype(F32)
        limit = jnp.repeat(kept[tokens : tokens + micro].astype(F32), window, axis=0)
        there = gather_x(jnp.stack([by_z, by_both]))
        there, previous, limit = lax.optimization_barrier((there, previous, limit))
        pieces = (near, side, there)

    first_own, first_other = own_of(first_rows, core), own_of(first_rows, 1 - core)

    def place(owns):
        table = jnp.stack(owns).reshape(len(owns), tokens, 2, piece)
        side = core ^ z_half
        mine = lax.dynamic_index_in_dim(table, side, 2, keepdims=False)
        theirs = swap_core(lax.dynamic_index_in_dim(table, 1 - side, 2, keepdims=False))
        return turn(ordered(core, mine, theirs, axis=2).reshape(len(owns), tokens, local))

    cot_chunks = jnp.pad(cot_chunks, ((0, 0), (0, SIDE), (0, 0)))
    cot_part, _ = back_call(flags, cot_chunks, pieces, False)
    cot_normed = gain_rows * (cot_part + swap_core(cot_part))

    own, following, other = first_own, first_own, first_other

    def norm_of(total):
        return lax.rsqrt(total / width + EPSILON)[:, None]

    for tick_no in range(sections):
        finished = tick_no == sections - 1
        rows = (following, other, first_own, first_other)
        outgoing = project_call(flags, rows, gain_rows, pieces, cot_normed if finished else None)
        received = exchange_quad(outgoing)
        rstd = norm_of(read_side(received[:, tokens:], tokens, 0))
        change = rstd * jnp.sum(received[:, :tokens].astype(F32), axis=0)
        result = own.astype(F32) + change
        if not finished:
            coded = jnp.clip(result - previous, -limit, limit).astype(BF16)
            following = hop((previous + coded.astype(F32)).astype(BF16), 1)
            own = jnp.where(is_first, first_own, following)
            other = swap_core(following)
        if tick_no == 1:
            other, cot_normed = lax.optimization_barrier((other, cot_normed))
    section_output = result.astype(BF16)

    stat = read_side(received[:, tokens:], tokens, SIDE // 2)[:, None] * rstd / width
    normed = own.astype(F32) * rstd
    last_grad = own_cotangent.astype(F32) + rstd * (own_of(cot_normed, core) - normed * stat)
    last_grad = last_grad.astype(BF16)

    last_rows = jnp.where(is_first, first_rows, rows_of(following, other)).astype(F32)
    hidden = (last_rows * rstd * gain_rows).astype(BF16)
    hidden = lax.dynamic_slice_in_dim(hidden, core * (tokens // 2), tokens // 2, 0)
    hidden_near, hidden_far = hidden[:, :local], swap_y(hidden[:, local:])

    grad_in = last_grad
    for tick_no in range(1, sections):
        moved = hop(grad_in, -1)
        if tick_no == 1:
            moved, hidden_far = lax.optimization_barrier((moved, hidden_far))
            hidden = ordered(y_half, hidden_near, hidden_far)
        upstream = jnp.where(is_last, own_cotangent, moved)
        if tick_no == sections - 1:
            sent = jnp.where(is_first, own_cotangent, grad_in).reshape(tokens, 2, piece)
            same = back_and_move(sent[:, 0], lambda z, x, c, h, q: pass_on(z, z, x, c, h, q))
            cross = back_and_move(sent[:, 1], lambda z, x, c, h, q: pass_on(z, 1 - z, x, c, h, q))
            columns = ordered(z_half, same, cross)
        values = upstream.astype(F32)
        side = side_rows([jnp.sum(values * change, axis=1)], 2 * piece)
        payload = jnp.concatenate([upstream, side], axis=0)
        gathered = exchange_quad(jnp.broadcast_to(payload[None], (quad, *payload.shape)))
        if tick_no == 1:
            gathered, hidden_far = lax.optimization_barrier((gathered, swap_z(hidden)))
            hidden = ordered(z_half, hidden, hidden_far)
        elif tick_no == 2:
            found = [hidden] + [shift_x(hidden, step) for step in range(1, ring)]
            gathered, found = lax.optimization_barrier((gathered, found))
            hidden = jnp.stack(found)
        elif tick_no == 3:
            gathered, hidden_far = lax.optimization_barrier((gathered, swap_core(hidden)))
            hidden = ordered(core, hidden, hidden_far, axis=3)
            order = [hidden[i, :, 0] for i in range(ring)]
            order += [hidden[ring - 1 - i, :, 1] for i in range(ring)]
            hidden = jnp.stack(order).reshape(ranks * tokens, local)
        part_mine, sent = back_call(flags, gathered, pieces, True)
        sum_mine = sent[tokens, :tokens]
        taken = swap_core(sent)
        stat = (sum_mine + taken[tokens, :tokens])[:, None] / width
        grad_normed = gain_own * (part_mine + taken[:tokens])
        grad_in = values + rstd * (grad_normed - normed * stat)
        grad_in = jnp.where(is_last, last_grad, grad_in.astype(BF16))
    placed = place([section_output, grad_in])

    with jax.named_scope("weight_grad"):
        columns = lax.all_to_all(
            jnp.broadcast_to(columns[None], (parts, *columns.shape)), "tensor", 0, 0
        ).reshape(ranks * tokens, piece)
        weight_grad = lax.dot_general(
            hidden, columns, (((0,), (0,)), ((), ())), preferred_element_type=F32
        )
    return placed[:1], placed[1:], weight_grad[None]


def solution(mesh):
    return jax.shard_map(
        body,
        mesh=mesh,
        in_specs=(
            P("dp", None),
            P("dp", None),
            P("section", "tensor", "dp"),
            P("section", None),
            P(None, "dp", None, "tensor"),
            P(None, "dp", "tensor"),
            P("dp"),
        ),
        out_specs=(
            P("section", "dp", "tensor"),
            P("section", "dp", "tensor"),
            P("section", "tensor", "dp"),
        ),
        check_vma=False,
    )
```

```python
import jax
import jax.numpy as jnp
from jax import lax
from jax.experimental import pallas as pl
from jax.experimental.pallas import tpu as pltpu
from jax.sharding import PartitionSpec as P

BLOCK = 32
EPSILON = 1e-05
SIDE = 16
VMEM_LIMIT = 12 * 1024 * 1024
F32 = jnp.float32
BF16 = jnp.bfloat16


def split_row(row, width):
    tokens = row.shape[1]
    high = row.astype(BF16).astype(F32)
    parts = [high, row - high]
    if width > 2 * tokens:
        parts.append(jnp.zeros((1, width - 2 * tokens), F32))
    return jnp.concatenate(parts, axis=1)


def token_row(table):
    tokens, width = table.shape
    folded = table[:, :tokens]
    for start in range(tokens, width, tokens):
        folded = folded + table[:, start : start + tokens]
    return jnp.sum(folded.T, axis=0, keepdims=True)


def weight_specs(pieces):
    last = pieces[0].shape[0] - 1
    shape = (1, *pieces[0].shape[1:])
    here = pl.BlockSpec(shape, lambda i, flags: (jnp.where(flags[3] == 0, i, last - i), 0, 0, 0))
    return [here, pl.BlockSpec(memory_space=pl.ANY)]


def far_scratch(pieces):
    return [pltpu.VMEM(pieces[1].shape, BF16), pltpu.SemaphoreType.DMA((pieces[1].shape[0],))]


def far_weights(flags, there, held, sems):
    step = pl.program_id(0)
    last = held.shape[0] - 1

    def copy(index):
        source = jnp.where(flags[3] == 0, last - index, index)
        return pltpu.make_async_copy(there.at[source], held.at[index], sems.at[index])

    @pl.when(step == 0)
    def _():
        for index in range(last + 1):
            copy(index).start()

    def wait():
        copy(step).wait()
        return held[step, 0], held[step, 1]

    return wait


def project_kernel(flags, mine, theirs, first_mine, first_theirs, gain, *refs):
    here, there = refs[:2]
    cot = refs[2] if len(refs) == 9 else None
    out, raw, scaled, sums, held, sems = refs[-6:]
    wait = far_weights(flags, there, held, sems)
    tokens, width = raw.shape
    local, piece = here.shape[-2:]
    first, core, flip = flags[0], flags[1], flags[2]

    @pl.when(pl.program_id(0) == 0)
    def _():
        for which, now, begin in ((core, mine, first_mine), (1 - core, theirs, first_theirs)):
            block = jnp.where(first == 1, begin[...], now[...])
            for half in range(2):
                start = pl.multiple_of(((half ^ flip) * 2 + which) * piece, piece)
                raw[:, pl.ds(start, piece)] = block[:, half * piece : (half + 1) * piece]
        values = raw[...].astype(F32)
        scaled[...] = (values * gain[...]).astype(BF16)
        upper = split_row(token_row(values * values), 2 * piece)
        lower = upper if cot is None else split_row(token_row(values * cot[...]), 2 * piece)
        index = lax.broadcasted_iota(jnp.int32, (SIDE, 2 * piece), 0)
        sums[...] = jnp.where(index < SIDE // 2, upper, lower).astype(BF16)

    def times(start, block):
        part = scaled[:, start : start + local]
        return jnp.dot(part, block, preferred_element_type=F32)

    out[0, :tokens, :piece] = (times(0, here[0, 0]) + times(local, here[0, 1])).astype(BF16)
    far, far_side = wait()
    out[0, :tokens, piece:] = (times(0, far) + times(local, far_side)).astype(BF16)
    out[0, tokens:, :] = sums[...]


def back_kernel(flags, chunk, here, there, *refs):
    total, sums, held, sems = refs[-4:]
    wait = far_weights(flags, there, held, sems)
    rows = total.shape[0]
    local, piece = here.shape[-2:]
    core, flip = flags[1], flags[2]
    step = pl.program_id(0)

    @pl.when(step == 0)
    def _():
        total[...] = jnp.zeros_like(total)
        sums[...] = jnp.zeros_like(sums)

    def times(part, block):
        return lax.dot_general(part, block, (((1,), (1,)), ((), ())), preferred_element_type=F32)

    low, high = chunk[0, :rows, :piece], chunk[0, :rows, piece:]
    far, far_side = wait()
    total[:, :local] += times(low, here[0, 0]) + times(high, far)
    total[:, local:] += times(low, here[0, 1]) + times(high, far_side)
    sums[...] += chunk[0, rows:, : 2 * rows].astype(F32)

    if len(refs) == 6:

        @pl.when(step == pl.num_programs(0) - 1)
        def _():
            mine, sent = refs[:2]
            for half in range(2):
                lanes = slice(half * piece, (half + 1) * piece)
                block = (half ^ flip) * 2
                start = pl.multiple_of((block + core) * piece, piece)
                mine[:, lanes] = total[:, pl.ds(start, piece)]
                start = pl.multiple_of((block + 1 - core) * piece, piece)
                sent[:rows, lanes] = total[:, pl.ds(start, piece)]
            both_parts = sums[:8, :rows] + sums[:8, rows:]
            sent[rows:, :rows] = both_parts
            if 2 * piece > rows:
                sent[rows:, rows:] = jnp.zeros((8, 2 * piece - rows), F32)


def whole_spec(value):
    return pl.BlockSpec(value.shape, lambda i, flags: (0,) * len(value.shape))


def project_call(flags, rows, gain, pieces, cot):
    tokens, own = rows[0].shape
    width = 2 * own
    ring, _, local, piece = pieces[0].shape
    operands = [*rows, gain, *pieces]
    specs = [whole_spec(value) for value in operands[:5]] + weight_specs(pieces)
    if cot is not None:
        operands.append(cot)
        specs.append(whole_spec(cot))
    return pl.pallas_call(
        project_kernel,
        grid_spec=pltpu.PrefetchScalarGridSpec(
            num_scalar_prefetch=1,
            grid=(ring,),
            in_specs=specs,
            out_specs=pl.BlockSpec((1, tokens + SIDE, 2 * piece), lambda i, flags: (i, 0, 0)),
            scratch_shapes=[
                pltpu.VMEM((tokens, width), BF16),
                pltpu.VMEM((tokens, width), BF16),
                pltpu.VMEM((SIDE, 2 * piece), BF16),
                *far_scratch(pieces),
            ],
        ),
        out_shape=jax.ShapeDtypeStruct((ring, tokens + SIDE, 2 * piece), BF16),
        compiler_params=pltpu.CompilerParams(vmem_limit_bytes=VMEM_LIMIT),
        cost_estimate=pl.CostEstimate(
            flops=4 * tokens * width * piece * ring,
            bytes_accessed=2 * width * 2 * piece * ring,
            transcendentals=0,
        ),
    )(flags, *operands)


def back_call(flags, chunks, pieces, split):
    ring, _, local, piece = pieces[0].shape
    tokens = chunks.shape[1] - SIDE
    total = jax.ShapeDtypeStruct((tokens, 2 * local), F32)
    sums = jax.ShapeDtypeStruct((SIDE, 2 * tokens), F32)
    mine = jax.ShapeDtypeStruct((tokens, 2 * piece), F32)
    sent = jax.ShapeDtypeStruct((tokens + 8, 2 * piece), F32)
    outs = [mine, sent] if split else [total, sums]
    held = [total, sums] if split else []
    return pl.pallas_call(
        back_kernel,
        grid_spec=pltpu.PrefetchScalarGridSpec(
            num_scalar_prefetch=1,
            grid=(ring,),
            in_specs=[pl.BlockSpec((1, *chunks.shape[1:]), lambda i, flags: (i, 0, 0))]
            + weight_specs(pieces),
            out_specs=[whole_spec(value) for value in outs],
            scratch_shapes=[pltpu.VMEM(value.shape, F32) for value in held] + far_scratch(pieces),
        ),
        out_shape=outs,
        compiler_params=pltpu.CompilerParams(vmem_limit_bytes=VMEM_LIMIT),
        cost_estimate=pl.CostEstimate(
            flops=8 * tokens * local * piece * ring,
            bytes_accessed=2 * local * 4 * piece * ring,
            transcendentals=0,
        ),
    )(flags, chunks, *pieces)


def side_rows(columns, width):
    rows = []
    for value in columns:
        high = lax.reduce_precision(value, 8, 7)
        pair = jnp.concatenate([high, value - high]).astype(BF16)
        rows.append(jnp.pad(pair, (0, width - pair.shape[0])))
    return jnp.pad(jnp.stack(rows), ((0, SIDE - len(rows)), (0, 0)))


def read_side(rows, tokens, row):
    pair = rows[:, row, : 2 * tokens].astype(F32)
    total = jnp.sum(pair, axis=0)
    return total[:tokens] + total[tokens:]


def ordered(flag, first, second, axis=0):
    return jnp.where(
        flag == 0, jnp.stack([first, second], axis), jnp.stack([second, first], axis)
    )


def body(inputs, cotangent, weights, gains, stored, scale_exp, example_ids):
    sections = lax.axis_size("section")
    ranks = lax.axis_size("dp")
    parts = lax.axis_size("tensor")
    section_pos = lax.axis_index("section")
    tensor_pos = lax.axis_index("tensor")
    dp_pos = lax.axis_index("dp")
    half = ranks // 2
    ring = half // 2
    quad = parts // 2
    z_half, x_pos, core = dp_pos // half, (dp_pos % half) // 2, dp_pos % 2
    y_half = tensor_pos // quad
    y_pos = jnp.where(y_half == 0, tensor_pos, parts - 1 - tensor_pos)
    flip = z_half ^ y_half
    tokens, width = inputs.shape
    local = weights.shape[1]
    piece = weights.shape[2]
    micro = example_ids.shape[0]
    window = tokens // micro
    bounds = stored.shape[0]
    is_first = section_pos == 0
    is_last = section_pos == sections - 1

    def rank_of(z, x, c):
        return z * half + x * 2 + c

    def row_of(h, q):
        return parts - 1 - q if h else q

    def quad_of(y):
        return (1, parts - 1 - y) if y >= quad else (0, y)

    def move(block, target):
        route = []
        for d in range(ranks):
            for y in range(parts):
                z, x, c, h, q = target(d // half, (d % half) // 2, d % 2, *quad_of(y))
                route.append((d * parts + y, rank_of(z, x, c) * parts + row_of(h, q)))
        return lax.ppermute(block, ("dp", "tensor"), route)

    def back_and_move(block, target):
        route = []
        for s in range(sections):
            for d in range(ranks):
                for y in range(parts):
                    z, x, c, h, q = target(d // half, (d % half) // 2, d % 2, *quad_of(y))
                    there = rank_of(z, x, c) * parts + row_of(h, q)
                    before = (s - 1) % sections
                    route.append(((s * ranks + d) * parts + y, before * ranks * parts + there))
        return lax.ppermute(block, ("section", "dp", "tensor"), route)

    def swap_z(block):
        return lax.ppermute(block, "dp", [(i, (i + half) % ranks) for i in range(ranks)])

    def swap_y(block):
        return lax.ppermute(block, "tensor", [(i, parts - 1 - i) for i in range(parts)])

    def swap_core(block):
        return lax.ppermute(block, "dp", [(i, i ^ 1) for i in range(ranks)])

    def turn(block):
        return move(block, lambda z, x, c, h, q: (z, x, h, c, q))

    def shift_x(block, step):
        route = [
            (rank_of(z, x, c), rank_of(z, (x + step) % ring, c))
            for z in range(2)
            for x in range(ring)
            for c in range(2)
        ]
        return lax.ppermute(block, "dp", route)

    def hop(block, step):
        devices = range(sections)
        return lax.ppermute(
            block, "section", [(i, i + step) for i in devices if i + step in devices]
        )

    def pass_on(z, to_z, x, c, h, q):
        to_x = ring - 1 - q if to_z else q
        return to_z, to_x, c, h, (to_x - x) % ring

    quads = [[row_of(h, i) for i in range(quad)] for h in range(2)]
    rings = [[rank_of(z, x, c) for x in range(ring)] for z in range(2) for c in range(2)]

    def exchange_quad(chunks):
        return lax.all_to_all(chunks, "tensor", 0, 0, axis_index_groups=quads)

    with jax.named_scope("weight_gather"):

        def gather_x(block):
            copies = jnp.broadcast_to(block[None], (ring, *block.shape))
            return lax.all_to_all(copies, "dp", 0, 0, axis_index_groups=rings)

        own_block = weights[0]
        by_y = swap_y(own_block)
        by_z = swap_z(own_block)
        by_both = swap_y(by_z)
        here = gather_x(jnp.stack([own_block, by_y]))
        by_both, here = lax.optimization_barrier((by_both, here))
    flags = jnp.stack([is_first.astype(jnp.int32), core, flip, z_half]).astype(jnp.int32)

    with jax.named_scope("layout"):
        native = core == y_half

        def blocks_of(rows):
            first = lax.dynamic_slice_in_dim(rows, tensor_pos * local, local, 1)
            second = lax.dynamic_slice_in_dim(rows, (parts - 1 - tensor_pos) * local, local, 1)
            return jnp.concatenate([first, second], axis=1)

        def columns_of(rows, which):
            table = rows.reshape(tokens, 2, ring, 2, piece)
            table = lax.dynamic_index_in_dim(table, which, 3, keepdims=False)
            low = jnp.stack([table[:, 0, i] for i in range(ring)])
            high = jnp.stack([table[:, 1, ring - 1 - i] for i in range(ring)])
            return ordered(z_half, low, high, axis=2).reshape(ring, tokens, 2 * piece)

        handed = (blocks_of(inputs), columns_of(cotangent, 1 - core))
        route = [
            (rank_of(z, x, h) * parts + row_of(h, q), rank_of(z, x, 1 - h) * parts + row_of(h, q))
            for z in range(2)
            for x in range(ring)
            for h in range(2)
            for q in range(quad)
        ]
        handed = [lax.ppermute(value, ("dp", "tensor"), route) for value in handed]
        first_rows = jnp.where(native, blocks_of(inputs), handed[0])
        cot_chunks = jnp.where(native, columns_of(cotangent, core), handed[1])
        own_cotangent = lax.dynamic_index_in_dim(cot_chunks, y_pos, 0, keepdims=False)

        def turned(table):
            return jnp.where(flip == 0, table, jnp.concatenate([table[:, 1:], table[:, :1]], axis=1))

        def own_of(rows, which):
            table = rows.reshape(rows.shape[0], 2, 2, piece)
            table = lax.dynamic_index_in_dim(table, which, 2, keepdims=False)
            return turned(table).reshape(rows.shape[0], 2 * piece)

        def rows_of(mine, other):
            table = ordered(
                core, mine.reshape(tokens, 2, piece), other.reshape(tokens, 2, piece), axis=2
            )
            return turned(table).reshape(tokens, 2 * local)

        gain_rows = blocks_of(gains).astype(F32)
        gain_own = own_of(gain_rows, core)

        bound = jnp.clip(section_pos, 0, bounds - 1)

        def chosen(table):
            return jnp.take(
                lax.dynamic_index_in_dim(table, bound, 0, keepdims=False), example_ids, axis=0
            )

        kept = chosen(stored).reshape(tokens, local)
        limit = jnp.repeat(jnp.exp2(chosen(scale_exp).astype(F32)), BLOCK, axis=1).astype(BF16)
        kept = jnp.concatenate([kept, jnp.pad(limit, ((0, SIDE - micro), (0, 0)))], axis=0)
        here, kept = lax.optimization_barrier((here, kept))
        kept = turn(kept).reshape(tokens + SIDE, 2, piece)
        mine = lax.dynamic_index_in_dim(kept, core, 1, keepdims=False)
        theirs = swap_core(lax.dynamic_index_in_dim(kept, 1 - core, 1, keepdims=False))
        kept = ordered(core ^ z_half, mine, theirs, axis=1).reshape(tokens + SIDE, 2 * piece)
        previous = kept[:tokens].astype(F32)
        limit = jnp.repeat(kept[tokens : tokens + micro].astype(F32), window, axis=0)
        there = gather_x(jnp.stack([by_z, by_both]))
        there, previous, limit = lax.optimization_barrier((there, previous, limit))
        pieces = (here, there)

    first_own, first_other = own_of(first_rows, core), own_of(first_rows, 1 - core)

    def place(owns):
        table = jnp.stack(owns).reshape(len(owns), tokens, 2, piece)
        side = core ^ z_half
        mine = lax.dynamic_index_in_dim(table, side, 2, keepdims=False)
        theirs = swap_core(lax.dynamic_index_in_dim(table, 1 - side, 2, keepdims=False))
        return turn(ordered(core, mine, theirs, axis=2).reshape(len(owns), tokens, local))

    cot_chunks = jnp.pad(cot_chunks, ((0, 0), (0, SIDE), (0, 0)))
    cot_part, _ = back_call(flags, cot_chunks, pieces, False)
    cot_normed = gain_rows * (cot_part + swap_core(cot_part))

    own, following, other = first_own, first_own, first_other

    def norm_of(total):
        return lax.rsqrt(total / width + EPSILON)[:, None]

    for tick_no in range(sections):
        finished = tick_no == sections - 1
        rows = (following, other, first_own, first_other)
        outgoing = project_call(flags, rows, gain_rows, pieces, cot_normed if finished else None)
        received = exchange_quad(outgoing)
        rstd = norm_of(read_side(received[:, tokens:], tokens, 0))
        change = rstd * jnp.sum(received[:, :tokens].astype(F32), axis=0)
        result = own.astype(F32) + change
        if not finished:
            coded = jnp.clip(result - previous, -limit, limit).astype(BF16)
            following = hop((previous + coded.astype(F32)).astype(BF16), 1)
            own = jnp.where(is_first, first_own, following)
            other = swap_core(following)
        if tick_no == 1:
            other, cot_normed = lax.optimization_barrier((other, cot_normed))
    section_output = result.astype(BF16)

    stat = read_side(received[:, tokens:], tokens, SIDE // 2)[:, None] * rstd / width
    normed = own.astype(F32) * rstd
    last_grad = own_cotangent.astype(F32) + rstd * (own_of(cot_normed, core) - normed * stat)
    last_grad = last_grad.astype(BF16)

    last_rows = jnp.where(is_first, first_rows, rows_of(following, other)).astype(F32)
    hidden = (last_rows * rstd * gain_rows).astype(BF16)
    hidden = lax.dynamic_slice_in_dim(hidden, core * (tokens // 2), tokens // 2, 0)
    hidden_near, hidden_far = hidden[:, :local], swap_y(hidden[:, local:])

    grad_in = last_grad
    for tick_no in range(1, sections):
        moved = hop(grad_in, -1)
        if tick_no == 1:
            moved, hidden_far = lax.optimization_barrier((moved, hidden_far))
            hidden = ordered(y_half, hidden_near, hidden_far)
        upstream = jnp.where(is_last, own_cotangent, moved)
        if tick_no == sections - 1:
            sent = jnp.where(is_first, own_cotangent, grad_in).reshape(tokens, 2, piece)
            same = back_and_move(sent[:, 0], lambda z, x, c, h, q: pass_on(z, z, x, c, h, q))
            cross = back_and_move(sent[:, 1], lambda z, x, c, h, q: pass_on(z, 1 - z, x, c, h, q))
            columns = ordered(z_half, same, cross)
        values = upstream.astype(F32)
        side = side_rows([jnp.sum(values * change, axis=1)], 2 * piece)
        payload = jnp.concatenate([upstream, side], axis=0)
        gathered = exchange_quad(jnp.broadcast_to(payload[None], (quad, *payload.shape)))
        if tick_no == 1:
            gathered, hidden_far = lax.optimization_barrier((gathered, swap_z(hidden)))
            hidden = ordered(z_half, hidden, hidden_far)
        elif tick_no == 2:
            found = [hidden] + [shift_x(hidden, step) for step in range(1, ring)]
            gathered, found = lax.optimization_barrier((gathered, found))
            hidden = jnp.stack(found)
        elif tick_no == 3:
            gathered, hidden_far = lax.optimization_barrier((gathered, swap_core(hidden)))
            hidden = ordered(core, hidden, hidden_far, axis=3)
            order = [hidden[i, :, 0] for i in range(ring)]
            order += [hidden[ring - 1 - i, :, 1] for i in range(ring)]
            hidden = jnp.stack(order).reshape(ranks * tokens, local)
        part_mine, sent = back_call(flags, gathered, pieces, True)
        sum_mine = sent[tokens, :tokens]
        taken = swap_core(sent)
        stat = (sum_mine + taken[tokens, :tokens])[:, None] / width
        grad_normed = gain_own * (part_mine + taken[:tokens])
        grad_in = values + rstd * (grad_normed - normed * stat)
        grad_in = jnp.where(is_last, last_grad, grad_in.astype(BF16))
    placed = place([section_output, grad_in])

    with jax.named_scope("weight_grad"):
        columns = lax.all_to_all(
            jnp.broadcast_to(columns[None], (parts, *columns.shape)), "tensor", 0, 0
        ).reshape(ranks * tokens, piece)
        weight_grad = lax.dot_general(
            hidden, columns, (((0,), (0,)), ((), ())), preferred_element_type=F32
        )
    return placed[:1], placed[1:], weight_grad[None]


def solution(mesh):
    return jax.shard_map(
        body,
        mesh=mesh,
        in_specs=(
            P("dp", None),
            P("dp", None),
            P("section", "tensor", "dp"),
            P("section", None),
            P(None, "dp", None, "tensor"),
            P(None, "dp", "tensor"),
            P("dp"),
        ),
        out_specs=(
            P("section", "dp", "tensor"),
            P("section", "dp", "tensor"),
            P("section", "tensor", "dp"),
        ),
        check_vma=False,
    )
```
